32 devices in a mesh: sec: 4 (over x, core), pts: 8 (over z, y).
Axes of the slice: x: 2, y: 2, z: 4, core: 2. Of those that a mesh axis runs over, the one named last changes fastest.
Arguments:
- points: bfloat16 [4, 8192, 1024], P('sec', 'pts'), may hold values from -10 to 10
- counts: int32 [4, 8], P('sec', 'pts'), may hold values from 256 to 1024, as said below
- input_gain: float32 [4, 1024], P('sec'), may hold values from 0.1 to 1.9
- key_weight: bfloat16 [4, 1024, 1024], P('sec', 'pts'), may hold values from -0.25 to 0.25
- value_weight: bfloat16 [4, 1024, 1024], P('sec', 'pts'), may hold values from -0.25 to 0.25
- query_weight: bfloat16 [1024, 1024], replicated, may hold values from -0.1875 to 0.1875
- output_weight: bfloat16 [1024, 1024], replicated, may hold values from -0.75 to 0.75
- middle_gain: float32 [1024], replicated, may hold values from 0.1 to 1.9
- up_weight: bfloat16 [1024, 4096], P(None, 'sec'), may hold values from -0.1875 to 0.1875
- down_weight: bfloat16 [4096, 1024], P('sec'), may hold values from -0.09375 to 0.09375
Outputs:
- updated: bfloat16 [8192, 1024], P('pts', 'sec')
The draws below stay inside these ranges and needn't reach their ends.
Inputs may be any that keep to these rules, and one draw needn't show every extreme that they name: `counts`: each block has 1024 slots; in every section some block is full.
All inputs are finite; a program needn't handle non-finite values.
Results may differ from the reference program's by a relative error of at most 0.0049.
Values may be sent and summed in bfloat16 or wider, within the bound.
A program may use at most 128 MiB of HBM per device.

```python
import jax
import jax.numpy as jnp
from jax import lax

HEADS = 8
HEAD_DIM = 128
D = 1024
FF = 4096
ROWS = 1024
PTS = 8192
N_SEC = 4


def draw_points(key, part):
    base_key, shift_key = jax.random.split(jax.random.fold_in(key, 11))
    region = ROWS // 4
    regions = PTS // region
    base = jnp.clip(jax.random.normal(base_key, (4, PTS, D), jnp.float32), -4.0, 4.0)
    spread = 1.5
    offsets = jnp.clip(jax.random.normal(shift_key, (4, regions, D), jnp.float32), -3.0, 3.0) * spread
    return (base + jnp.repeat(offsets, region, axis=1)).astype(jnp.bfloat16)


def draw_counts(key, part):
    fill_key, spot_key = jax.random.split(jax.random.fold_in(key, 23))
    blocks = PTS // ROWS
    values = jax.random.randint(fill_key, (4, blocks), ROWS // 4, ROWS + 1)
    spots = jax.random.randint(spot_key, (4, 1), 0, blocks)
    full = jnp.arange(blocks)[None, :] == spots
    return jnp.where(full, ROWS, values).astype(jnp.int32)


def strengthened(entries, rng, source, target, parts, factor):
    owner, partner = [(jnp.arange(entries.shape[dim]) // (entries.shape[dim] // parts)).reshape([-1 if axis == dim else 1 for axis in range(entries.ndim)]) for dim in (source, target)]
    chosen = jax.random.permutation(rng, parts)[partner]
    strong = (owner == chosen) | (owner == (partner + parts // 2) % parts)
    return jnp.where(strong, factor * entries, entries)


def level_of(own_key, shape, shards, smallest, largest):
    factor_of = 1.0
    for axis_at, parts in shards:
        draws = jax.random.uniform(jax.random.fold_in(jax.random.fold_in(own_key, 6), axis_at), (parts,), jnp.float32, smallest / len(shards), largest / len(shards))
        factor_of = factor_of * jnp.repeat(jnp.exp(draws), shape[axis_at] // parts).reshape((-1,) + (1,) * (len(shape) - 1 - axis_at))
    return factor_of


def scatter_about(own_key, extent, scale, bound, cuts=(), held_as=jnp.bfloat16):
    entries = scale * jax.random.normal(own_key, extent, jnp.float32)
    if cuts:
        entries = entries * level_of(own_key, extent, cuts, -0.22, 0.18)
    return jnp.clip(entries, -bound, bound).astype(held_as)


def gaussian_with(stream_key, extent, scale, most, cuts, heavy, held_as=jnp.bfloat16):
    result = scale * jax.random.normal(stream_key, extent, jnp.float32)
    if cuts:
        result = result * level_of(stream_key, extent, cuts, -0.22, 0.18)
    return jnp.clip(strengthened(result, jax.random.fold_in(stream_key, 3), *heavy), -most, most).astype(held_as)


def setup_inputs(seed: int = 0) -> dict:
    arg_keys = jax.random.split(jax.random.key(seed), 11)
    return {
        "points": draw_points(jax.random.fold_in(arg_keys[10], 71), 0),
        "counts": draw_counts(jax.random.fold_in(arg_keys[10], 71), 0),
        "input_gain": jnp.clip(1.0 + 0.18 * jax.random.normal(arg_keys[2], (N_SEC, D), jnp.float32), 0.1, 1.9),
        "key_weight": gaussian_with(arg_keys[3], (N_SEC, D, D), D ** -0.5, 0.25, ((0, 4), (1, 8)), (1, 2, 8, 2.0)),
        "value_weight": gaussian_with(arg_keys[4], (N_SEC, D, D), D ** -0.5, 0.25, ((0, 4), (1, 8)), (1, 2, 8, 2.0)),
        "query_weight": scatter_about(arg_keys[5], (D, D), D ** -0.5, 0.1875),
        "output_weight": scatter_about(arg_keys[6], (D, D), (D // 16) ** -0.5, 0.75),
        "middle_gain": jnp.clip(1.0 + 0.18 * jax.random.normal(arg_keys[7], (D,), jnp.float32), 0.1, 1.9),
        "up_weight": scatter_about(arg_keys[8], (D, FF), D ** -0.5, 0.1875, ((1, 4),)),
        "down_weight": scatter_about(arg_keys[9], (FF, D), FF ** -0.5, 0.09375, ((0, 4),)),
    }


def layer_normalizer(values, gain):
    mean = lax.optimization_barrier(jnp.mean(values, axis=-1, keepdims=True))
    centred = values - mean
    spread = lax.optimization_barrier(jnp.mean(centred * centred, axis=-1, keepdims=True))
    return centred * lax.rsqrt(spread + 1e-05) * gain

def feature_map(values):
    return jax.nn.elu(values) + 1.0

def reference(points, counts, input_gain, key_weight, value_weight, query_weight, output_weight, middle_gain, up_weight, down_weight):
    sections = points.shape[0]
    slot_index = (jnp.arange(PTS) % ROWS).astype(jnp.int32)
    valid = slot_index[None, :] < jnp.repeat(counts, ROWS, axis=1)
    query_normed = layer_normalizer(points[sections - 1].astype(jnp.float32), input_gain[sections - 1]).astype(jnp.bfloat16)
    query_feats = feature_map(jnp.dot(query_normed, query_weight, preferred_element_type=jnp.float32)).astype(jnp.bfloat16)
    query_feats = lax.optimization_barrier(query_feats)
    per_head_queries = query_feats.astype(jnp.float32).reshape(PTS, HEADS, HEAD_DIM)
    attended = jnp.zeros((PTS, HEADS, HEAD_DIM), jnp.float32)
    for section in range(sections):
        normed = layer_normalizer(points[section].astype(jnp.float32), input_gain[section]).astype(jnp.bfloat16)
        key_feats = feature_map(jnp.dot(normed, key_weight[section], preferred_element_type=jnp.float32)).astype(jnp.bfloat16)
        key_feats = jnp.where(valid[section][:, None], key_feats, jnp.zeros_like(key_feats))
        value_rows = jnp.dot(normed, value_weight[section], preferred_element_type=jnp.float32).astype(jnp.bfloat16)
        per_head_keys = key_feats.astype(jnp.float32).reshape(PTS, HEADS, HEAD_DIM)
        per_head_values = value_rows.astype(jnp.float32).reshape(PTS, HEADS, HEAD_DIM)
        state_matrices = jnp.einsum('yzl,yzn->zln', per_head_keys, per_head_values)
        totals = lax.optimization_barrier(jnp.sum(per_head_keys, axis=0))
        numerator = jnp.einsum('upz,pzm->upm', per_head_queries, state_matrices, precision=lax.Precision.HIGHEST)
        denom = jnp.einsum('rhk,hk->rh', per_head_queries, totals, precision=lax.Precision.HIGHEST)
        attended = attended + numerator / denom[:, :, None]
    attended = attended.reshape(PTS, HEADS * HEAD_DIM).astype(jnp.bfloat16)
    mixed = points[sections - 1].astype(jnp.float32) + jnp.dot(attended, output_weight, preferred_element_type=jnp.float32)
    centred = layer_normalizer(mixed, middle_gain).astype(jnp.bfloat16)
    hidden = jax.nn.gelu(jnp.dot(centred, up_weight, preferred_element_type=jnp.float32), approximate=True).astype(jnp.bfloat16)
    return (mixed + jnp.dot(hidden, down_weight, preferred_element_type=jnp.float32)).astype(jnp.bfloat16)
```

```python
import functools

import jax
import jax.numpy as jnp
from jax import lax
from jax.experimental import pallas as pl
from jax.experimental.pallas import tpu as pltpu
from jax.sharding import PartitionSpec as P

HEAD_DIM = 128
EXTRA = 16
MESH = pl.DeviceIdType.MESH
DMA = pltpu.SemaphoreType.DMA
VMEM_LIMIT = 48 * 1024 * 1024


def layer_normalizer(values, gain):
    mean = jnp.mean(values, axis=-1, keepdims=True)
    centred = values - mean
    spread = jnp.mean(centred * centred, axis=-1, keepdims=True)
    return centred * lax.rsqrt(spread + 1e-05) * gain


def feature_map(values):
    return jax.nn.elu(values) + 1.0


def sibling_of(sec):
    return sec + 1 - 2 * lax.rem(sec, 2)


def across_of(sec):
    return lax.rem(sec + 2, 4)


def remote(src, dst, send_sem, recv_sem, **where):
    return pltpu.make_async_remote_copy(
        src_ref=src,
        dst_ref=dst,
        send_sem=send_sem,
        recv_sem=recv_sem,
        device_id=where,
        device_id_type=MESH,
    )


def gather_kernel(
    blocks, sections, key_ref, value_ref, points_ref, gain_ref,
    wk_ref, wv_ref, query_ref, query_gain_ref,
    local_sem, up_sem, down_sem, pair_sem, line_recv, pair_recv, query_send, query_recv, gain_send, gain_recv,
):
    length = blocks // 2
    depth = key_ref.shape[0]
    share = query_ref.shape[0]
    sec = lax.axis_index("sec")
    me = lax.axis_index("pts")
    spot, side = me // 2, lax.rem(me, 2)
    pair = spot * 2 + 1 - side
    owner = sections - 1
    barrier = pltpu.get_barrier_semaphore()
    for other in (lax.rem(spot + 1, length) * 2 + side, lax.rem(spot + length - 1, length) * 2 + side, pair):
        pl.semaphore_signal(barrier, inc=1, device_id={"pts": other}, device_id_type=MESH)
    for step in range(1, sections):
        pl.semaphore_signal(
            barrier, inc=1, device_id={"sec": lax.rem(sec + step, sections)}, device_id_type=MESH
        )
    pl.semaphore_wait(barrier, 3 + sections - 1)

    def query_copy(to):
        return remote(
            points_ref.at[pl.ds(to * share, share)], query_ref, query_send.at[to], query_recv, sec=to
        )

    def gain_copy(to):
        return remote(gain_ref, query_gain_ref, gain_send.at[to], gain_recv, sec=to)

    def kept_query():
        return pltpu.make_async_copy(
            points_ref.at[pl.ds(owner * share, share)], query_ref, local_sem.at[2]
        )

    def kept_gain():
        return pltpu.make_async_copy(gain_ref, query_gain_ref, local_sem.at[3])

    @pl.when(sec == owner)
    def _():
        for to in range(owner):
            gain_copy(to).start()
            query_copy(to).start()
        kept_query().start()
        kept_gain().start()

    shards = (key_ref, value_ref)
    wholes = (wk_ref, wv_ref)

    def place(which, index):
        return wholes[which].at[pl.ds(pl.multiple_of(index * depth, depth), depth)]

    def line_copy(which, source, step, own):
        here = place(which, source * 2 + side)
        sems = up_sem if step > 0 else down_sem
        return remote(
            shards[which] if own else here, here, sems.at[which, source], line_recv.at[which, source],
            pts=(spot + step) * 2 + side,
        )

    def pair_copy(which, source, own):
        here = place(which, source * 2 + side)
        return remote(
            shards[which] if own else here, here, pair_sem.at[which, source], pair_recv.at[which, source],
            pts=pair,
        )

    def kept(which):
        return pltpu.make_async_copy(shards[which], place(which, me), local_sem.at[which])

    for which in range(2):
        @pl.when(spot < length - 1)
        def _():
            line_copy(which, spot, 1, True).start()

        @pl.when(spot > 0)
        def _():
            line_copy(which, spot, -1, True).start()

        pair_copy(which, spot, True).start()
    for which in range(2):
        kept(which).start()
    for distance in range(1, length):
        for which in range(2):
            @pl.when(spot - distance >= 0)
            def _():
                source = spot - distance
                line_copy(which, source, 1, False).wait_recv()

                @pl.when(spot < length - 1)
                def _():
                    line_copy(which, source, 1, False).start()

                pair_copy(which, source, False).start()

            @pl.when(spot + distance < length)
            def _():
                source = spot + distance
                line_copy(which, source, -1, False).wait_recv()

                @pl.when(spot > 0)
                def _():
                    line_copy(which, source, -1, False).start()

                pair_copy(which, source, False).start()

    for source in range(length):
        for which in range(2):
            there = place(which, source * 2 + 1 - side)
            remote(
                there, there, pair_sem.at[which, source], pair_recv.at[which, source], pts=pair
            ).wait_recv()
    for source in range(length):
        for which in range(2):
            pair_copy(which, source, False).wait_send()

            @pl.when(jnp.logical_and(spot < length - 1, source <= spot))
            def _():
                line_copy(which, source, 1, False).wait_send()

            @pl.when(jnp.logical_and(spot > 0, source >= spot))
            def _():
                line_copy(which, source, -1, False).wait_send()

    for which in range(2):
        kept(which).wait()

    @pl.when(sec == owner)
    def _():
        for to in range(owner):
            gain_copy(to).wait_send()
            query_copy(to).wait_send()
        kept_query().wait()
        kept_gain().wait()

    @pl.when(sec != owner)
    def _():
        gain_copy(0).wait_recv()
        query_copy(0).wait_recv()


def gather_projections(blocks, sections, key, value, points, gain):
    depth, width = key.shape
    rows = points.shape[0]
    length = blocks // 2
    anywhere = pl.BlockSpec(memory_space=pl.ANY)
    return pl.pallas_call(
        functools.partial(gather_kernel, blocks, sections),
        out_shape=(
            jax.ShapeDtypeStruct((depth * blocks, width), key.dtype),
            jax.ShapeDtypeStruct((depth * blocks, width), value.dtype),
            jax.ShapeDtypeStruct((rows // sections, width), points.dtype),
            jax.ShapeDtypeStruct(gain.shape, gain.dtype),
        ),
        in_specs=[anywhere] * 4,
        out_specs=(anywhere,) * 4,
        scratch_shapes=[
            DMA((4,)),
            DMA((2, length)),
            DMA((2, length)),
            DMA((2, length)),
            DMA((2, length)),
            DMA((2, length)),
            DMA((sections,)),
            DMA,
            DMA((sections,)),
            DMA,
        ],
        compiler_params=pltpu.CompilerParams(
            collective_id=0, has_side_effects=True, vmem_limit_bytes=VMEM_LIMIT
        ),
    )(key, value, points, gain)


def state_kernel(
    blocks, part_ref, out_ref, landed, part_send, part_recv, share_send, share_recv, across_send, across_recv,
    near_send, near_recv,
):
    sec = lax.axis_index("sec")
    me = lax.axis_index("pts")
    near, across = sibling_of(sec), across_of(sec)
    barrier = pltpu.get_barrier_semaphore()
    for step in range(1, blocks):
        pl.semaphore_signal(
            barrier, inc=1, device_id={"pts": lax.rem(me + step, blocks)}, device_id_type=MESH
        )
    for other in (near, across):
        pl.semaphore_signal(barrier, inc=1, device_id={"sec": other}, device_id_type=MESH)
    pl.semaphore_wait(barrier, blocks + 1)

    def part_copy(step):
        to = lax.rem(me + step, blocks)
        return remote(part_ref.at[to], landed.at[step], part_send.at[step], part_recv.at[step], pts=to)

    def share_copy(step):
        mine = out_ref.at[sec, me]
        return remote(mine, mine, share_send.at[step], share_recv.at[step], pts=lax.rem(me + step, blocks))

    def arriving(step):
        slot = out_ref.at[sec, lax.rem(me + blocks - step, blocks)]
        return remote(slot, slot, share_send.at[step], share_recv.at[step], pts=me)

    def across_copy(step):
        slot = out_ref.at[sec, lax.rem(me + blocks - step, blocks)]
        return remote(slot, slot, across_send.at[step], across_recv.at[step], sec=across)

    def across_arriving(step):
        slot = out_ref.at[across, lax.rem(me + blocks - step, blocks)]
        return remote(slot, slot, across_send.at[step], across_recv.at[step], sec=across)

    def near_copy(kind, step):
        slot = out_ref.at[across if kind else sec, lax.rem(me + blocks - step, blocks)]
        return remote(slot, slot, near_send.at[kind, step], near_recv.at[kind, step], sec=near)

    def near_arriving(kind, step):
        slot = out_ref.at[across_of(near) if kind else near, lax.rem(me + blocks - step, blocks)]
        return remote(slot, slot, near_send.at[kind, step], near_recv.at[kind, step], sec=near)

    for step in range(1, blocks):
        part_copy(step).start()
    total = part_ref[me].astype(jnp.float32)
    for step in range(1, blocks):
        part_copy(step).wait_recv()
        total += landed[step].astype(jnp.float32)
    out_ref[sec, me] = total.astype(out_ref.dtype)
    for step in range(1, blocks):
        share_copy(step).start()
    for step in range(blocks):
        if step:
            arriving(step).wait_recv()
        across_copy(step).start()
        near_copy(0, step).start()
    for step in range(blocks):
        across_arriving(step).wait_recv()
        near_copy(1, step).start()
    for step in range(blocks):
        near_arriving(0, step).wait_recv()
        near_arriving(1, step).wait_recv()
    for step in range(1, blocks):
        part_copy(step).wait_send()
        share_copy(step).wait_send()
    for step in range(blocks):
        across_copy(step).wait_send()
        near_copy(0, step).wait_send()
        near_copy(1, step).wait_send()


def sum_states(blocks, sections, parts):
    inside = pl.BlockSpec(memory_space=pltpu.VMEM)
    return pl.pallas_call(
        functools.partial(state_kernel, blocks),
        out_shape=jax.ShapeDtypeStruct((sections,) + parts.shape, parts.dtype),
        in_specs=[inside],
        out_specs=inside,
        scratch_shapes=[
            pltpu.VMEM(parts.shape, parts.dtype),
            DMA((blocks,)),
            DMA((blocks,)),
            DMA((blocks,)),
            DMA((blocks,)),
            DMA((blocks,)),
            DMA((blocks,)),
            DMA((2, blocks)),
            DMA((2, blocks)),
        ],
        compiler_params=pltpu.CompilerParams(
            collective_id=1, has_side_effects=True, vmem_limit_bytes=VMEM_LIMIT
        ),
    )(parts)


def feed_kernel(
    centred_ref, mixed_ref, up_ref, down_ref, out_ref,
    rows_in, sums, own, cross, to_near, from_near, to_across, from_across,
    gather_send, gather_recv, near_send, near_recv, across_send, across_recv,
):
    sec = lax.axis_index("sec")
    near, across = sibling_of(sec), across_of(sec)
    corner = sibling_of(across)
    share = centred_ref.shape[0]
    columns = out_ref.shape[1]
    barrier = pltpu.get_barrier_semaphore()
    for other in (near, across):
        pl.semaphore_signal(barrier, inc=1, device_id={"sec": other}, device_id_type=MESH)
    pl.semaphore_wait(barrier, 2)

    to_x = remote(centred_ref, rows_in.at[sec], gather_send.at[0], gather_recv.at[sec], sec=across)
    to_n = remote(centred_ref, rows_in.at[sec], gather_send.at[1], gather_recv.at[sec], sec=near)
    pass_on = remote(rows_in.at[across], rows_in.at[across], gather_send.at[2], gather_recv.at[across], sec=near)

    def landing(block):
        return remote(rows_in.at[block], rows_in.at[block], gather_send.at[2], gather_recv.at[block], sec=near)

    def near_copy(block):
        return remote(to_near.at[block], from_near.at[block], near_send.at[block], near_recv.at[block], sec=near)

    def across_copy(block):
        return remote(
            to_across.at[block], from_across.at[block], across_send.at[block], across_recv.at[block], sec=across
        )

    to_x.start()
    to_n.start()
    span = 256
    steps = up_ref.shape[1] // span

    def run(source, first):
        if first:
            sums[...] = mixed_ref[...]
        else:
            sums[...] = jnp.zeros_like(sums)

        @pl.loop(0, steps)
        def _(step):
            units = pl.ds(pl.multiple_of(step * span, span), span)
            hidden = jax.nn.gelu(
                jnp.dot(source[...], up_ref[:, units], preferred_element_type=jnp.float32), approximate=True
            ).astype(jnp.bfloat16)
            sums[...] += jnp.dot(hidden, down_ref[units, :], preferred_element_type=jnp.float32)

    def part(of):
        return sums[:, pl.ds(pl.multiple_of(of * columns, columns), columns)]

    low = lax.rem(near, 2)

    def emit(block):
        own[block] = part(sec)
        cross[block] = part(across)
        to_near[block, 0] = part(low).astype(jnp.bfloat16)
        to_near[block, 1] = part(low + 2).astype(jnp.bfloat16)
        near_copy(block).start()

    def forward(block):
        near_copy(block).wait_recv()
        to_across[block] = (cross[block] + from_near[block, across // 2].astype(jnp.float32)).astype(jnp.bfloat16)
        across_copy(block).start()

    run(centred_ref, True)
    emit(sec)
    landing(near).wait_recv()
    run(rows_in.at[near], False)
    emit(near)
    forward(near)
    forward(sec)
    landing(across).wait_recv()
    pass_on.start()
    run(rows_in.at[across], False)
    emit(across)
    landing(corner).wait_recv()
    run(rows_in.at[corner], False)
    emit(corner)
    forward(corner)
    forward(across)
    for block in (near, sec, corner, across):
        across_copy(block).wait_recv()
        out_ref[pl.ds(pl.multiple_of(block * share, share), share), :] = (
            own[block] + from_near[block, sec // 2].astype(jnp.float32) + from_across[block].astype(jnp.float32)
        ).astype(out_ref.dtype)
    for block in (near, sec, corner, across):
        near_copy(block).wait_send()
        across_copy(block).wait_send()
    to_x.wait_send()
    to_n.wait_send()
    pass_on.wait_send()


def feed_forward(sections, centred, mixed, up, down):
    share, width = centred.shape
    columns = width // sections
    inside = pl.BlockSpec(memory_space=pltpu.VMEM)
    half = jnp.bfloat16
    return pl.pallas_call(
        feed_kernel,
        out_shape=jax.ShapeDtypeStruct((share * sections, columns), half),
        in_specs=[inside] * 4,
        out_specs=inside,
        scratch_shapes=[
            pltpu.VMEM((sections, share, width), half),
            pltpu.VMEM((share, width), jnp.float32),
            pltpu.VMEM((sections, share, columns), jnp.float32),
            pltpu.VMEM((sections, share, columns), jnp.float32),
            pltpu.VMEM((sections, 2, share, columns), half),
            pltpu.VMEM((sections, 2, share, columns), half),
            pltpu.VMEM((sections, share, columns), half),
            pltpu.VMEM((sections, share, columns), half),
            DMA((3,)),
            DMA((sections,)),
            DMA((sections,)),
            DMA((sections,)),
            DMA((sections,)),
            DMA((sections,)),
        ],
        compiler_params=pltpu.CompilerParams(
            collective_id=2, has_side_effects=True, vmem_limit_bytes=VMEM_LIMIT
        ),
    )(centred, mixed, up, down)


def on_device(
    points,
    counts,
    input_gain,
    key_weight,
    value_weight,
    query_weight,
    output_weight,
    middle_gain,
    up_weight,
    down_weight,
):
    block = points[0]
    rows, width = block.shape
    heads = width // HEAD_DIM
    sections = lax.axis_size("sec")
    blocks = lax.axis_size("pts")
    whole_key, whole_value, query_rows, query_gain = gather_projections(
        blocks, sections, key_weight[0], value_weight[0], block, input_gain.reshape(heads, HEAD_DIM)
    )
    normed = layer_normalizer(block.astype(jnp.float32), input_gain[0]).astype(jnp.bfloat16)
    valid = jnp.arange(rows) < counts[0, 0]
    key_feats = feature_map(
        jnp.dot(normed, whole_key, preferred_element_type=jnp.float32)
    ).astype(jnp.bfloat16)
    key_feats = jnp.where(valid[:, None], key_feats, jnp.zeros_like(key_feats))
    value_rows = jnp.dot(normed, whole_value, preferred_element_type=jnp.float32).astype(jnp.bfloat16)
    local_state = jnp.einsum(
        "yzl,yzn->zln",
        key_feats.reshape(rows, heads, HEAD_DIM),
        value_rows.reshape(rows, heads, HEAD_DIM),
        preferred_element_type=jnp.float32,
    ).reshape(width, HEAD_DIM)
    local_total = jnp.sum(key_feats.astype(jnp.float32), axis=0)
    slab = width // blocks
    extra = jnp.pad(local_total.reshape(blocks, 1, slab), ((0, 0), (0, EXTRA - 1), (0, HEAD_DIM - slab)))
    parts = jnp.concatenate([local_state.reshape(blocks, slab, HEAD_DIM), extra], axis=1).astype(jnp.bfloat16)
    summed = sum_states(blocks, sections, parts)
    state_heads = summed[:, :, :slab].reshape(sections, heads, HEAD_DIM, HEAD_DIM)
    total_heads = summed[:, :, slab, :slab].reshape(sections, heads, HEAD_DIM)

    query_wide = query_rows.astype(jnp.float32)
    query_normed = layer_normalizer(query_wide, query_gain.reshape(width)).astype(jnp.bfloat16)
    query_feats = feature_map(
        jnp.dot(query_normed, query_weight, preferred_element_type=jnp.float32)
    ).astype(jnp.bfloat16)
    share = query_rows.shape[0]
    per_head_queries = query_feats.reshape(share, heads, HEAD_DIM)
    numerator = jnp.einsum(
        "rhk,shkv->srhv", per_head_queries, state_heads, preferred_element_type=jnp.float32
    )
    denom = jnp.einsum("rhk,shk->srh", per_head_queries, total_heads, preferred_element_type=jnp.float32)
    attended = (
        jnp.sum(numerator / denom[:, :, :, None], axis=0).reshape(share, width).astype(jnp.bfloat16)
    )
    mixed = query_wide + jnp.dot(attended, output_weight, preferred_element_type=jnp.float32)
    centred = layer_normalizer(mixed, middle_gain).astype(jnp.bfloat16)
    return feed_forward(sections, centred, mixed, up_weight, down_weight)


def solution(mesh):
    placed = (
        P("sec", "pts", None),
        P("sec", "pts"),
        P("sec", None),
        P("sec", "pts", None),
        P("sec", "pts", None),
        P(),
        P(),
        P(),
        P(None, "sec"),
        P("sec", None),
    )
    return jax.shard_map(
        on_device, mesh=mesh, in_specs=placed, out_specs=P("pts", "sec"), check_vma=False
    )
```

```python
import functools

import jax
import jax.numpy as jnp
from jax import lax
from jax.experimental import pallas as pl
from jax.experimental.pallas import tpu as pltpu
from jax.sharding import PartitionSpec as P

HEAD_DIM = 128
EXTRA = 16
MESH = pl.DeviceIdType.MESH
DMA = pltpu.SemaphoreType.DMA
VMEM_LIMIT = 48 * 1024 * 1024


def layer_normalizer(values, gain):
    mean = jnp.mean(values, axis=-1, keepdims=True)
    centred = values - mean
    spread = jnp.mean(centred * centred, axis=-1, keepdims=True)
    return centred * lax.rsqrt(spread + 1e-05) * gain


def feature_map(values):
    return jax.nn.elu(values) + 1.0


def sibling_of(sec):
    return sec + 1 - 2 * lax.rem(sec, 2)


def across_of(sec):
    return lax.rem(sec + 2, 4)


def remote(src, dst, send_sem, recv_sem, **where):
    return pltpu.make_async_remote_copy(
        src_ref=src,
        dst_ref=dst,
        send_sem=send_sem,
        recv_sem=recv_sem,
        device_id=where,
        device_id_type=MESH,
    )


def gather_kernel(
    blocks, sections, shard_ref, points_ref, aux_ref,
    whole_ref, rows_ref, rows_aux_ref, query_ref, query_aux_ref,
    local_sem, up_sem, down_sem, near_sem, pair_sem, recv_sem, swap_send, swap_recv, query_send, query_recv,
):
    length = blocks // 2
    depth = shard_ref.shape[1]
    share = query_ref.shape[0]
    sec = lax.axis_index("sec")
    me = lax.axis_index("pts")
    spot, side = me // 2, lax.rem(me, 2)
    core = lax.rem(sec, 2)
    base = sec - core
    near = base + 1 - core
    pair = spot * 2 + 1 - side
    owner = sections - 1
    barrier = pltpu.get_barrier_semaphore()

    def greet(**where):
        pl.semaphore_signal(barrier, inc=1, device_id=where, device_id_type=MESH)

    for other in (near, across_of(sec), across_of(near)):
        greet(sec=other)
    for step in (1, length - 1):
        beside = lax.rem(spot + step, length) * 2 + side
        greet(pts=beside)
        greet(sec=near, pts=beside)
    greet(pts=pair)
    greet(sec=near, pts=pair)
    pl.semaphore_wait(barrier, 9)

    def place(which, index):
        return whole_ref.at[which, pl.ds(pl.multiple_of(index * depth, depth), depth)]

    def copy(which, index, sem, own, **where):
        here = place(which, index)
        return remote(
            shard_ref.at[which] if own else here, here, sem.at[which, index], recv_sem.at[which, index], **where
        )

    def line_copy(which, index, step, own=False):
        where = {"sec": base + which, "pts": me + 2 * step} if own else {"pts": me + 2 * step}
        return copy(which, index, up_sem if step > 0 else down_sem, own, **where)

    def near_copy(which, index, own=False):
        return copy(which, index, near_sem, own, sec=near)

    def pair_copy(which):
        return copy(which, me, pair_sem, True, sec=base + which, pts=pair)

    def kept(which):
        return pltpu.make_async_copy(shard_ref.at[which], place(which, me), local_sem.at[which])

    swap_to = {"sec": base + side, "pts": spot * 2 + core}

    def swap_rows():
        return remote(points_ref, rows_ref, swap_send.at[0], swap_recv.at[0], **swap_to)

    def swap_aux():
        return remote(aux_ref, rows_aux_ref, swap_send.at[1], swap_recv.at[1], **swap_to)

    def kept_rows():
        return pltpu.make_async_copy(points_ref, rows_ref, local_sem.at[2])

    def kept_aux():
        return pltpu.make_async_copy(aux_ref, rows_aux_ref, local_sem.at[3])

    def query_copy(to):
        return remote(
            points_ref.at[pl.ds(to % 2 * share, share)], query_ref, query_send.at[0, to], query_recv.at[0], sec=to
        )

    def query_aux(to):
        return remote(aux_ref, query_aux_ref, query_send.at[1, to], query_recv.at[1], sec=to)

    def kept_query():
        return pltpu.make_async_copy(points_ref.at[pl.ds(owner % 2 * share, share)], query_ref, local_sem.at[4])

    def kept_query_aux():
        return pltpu.make_async_copy(aux_ref, query_aux_ref, local_sem.at[5])

    @pl.when(core != side)
    def _():
        for which in range(2):
            pair_copy(which).start()

    @pl.when(core == side)
    def _():
        for which in range(2):
            @pl.when(spot < length - 1)
            def _():
                line_copy(which, me, 1, True).start()

            @pl.when(spot > 0)
            def _():
                line_copy(which, me, -1, True).start()

            near_copy(which, me, True).start()
            kept(which).start()

    @pl.when(core != side)
    def _():
        swap_aux().start()
        swap_rows().start()

    @pl.when(core == side)
    def _():
        kept_aux().start()
        kept_rows().start()

    @pl.when(sec == owner)
    def _():
        for to in range(owner):
            query_aux(to).start()
            query_copy(to).start()
        kept_query().start()
        kept_query_aux().start()

    def arrive(index, up, down):
        copy(core, index, near_sem, False, sec=near).wait_recv()
        if up:
            @pl.when(spot < length - 1)
            def _():
                line_copy(core, index, 1).start()
        if down:
            @pl.when(spot > 0)
            def _():
                line_copy(core, index, -1).start()
        near_copy(core, index).start()

    arrive(pair, True, True)
    for distance in range(1, length):
        for other in range(2):
            column = side if other == 0 else 1 - side

            @pl.when(spot - distance >= 0)
            def _():
                arrive((spot - distance) * 2 + column, True, False)

            @pl.when(spot + distance < length)
            def _():
                arrive((spot + distance) * 2 + column, False, True)

    for index in range(blocks):
        @pl.when(index != me)
        def _():
            near_copy(1 - core, index).wait_recv()
            near_copy(core, index).wait_send()

            @pl.when(jnp.logical_and(spot < length - 1, index // 2 <= spot))
            def _():
                line_copy(core, index, 1).wait_send()

            @pl.when(jnp.logical_and(spot > 0, index // 2 >= spot))
            def _():
                line_copy(core, index, -1).wait_send()

    @pl.when(core == side)
    def _():
        for which in range(2):
            @pl.when(spot < length - 1)
            def _():
                line_copy(which, me, 1, True).wait_send()

            @pl.when(spot > 0)
            def _():
                line_copy(which, me, -1, True).wait_send()

            near_copy(which, me, True).wait_send()
            kept(which).wait()
        kept_aux().wait()
        kept_rows().wait()

    @pl.when(core != side)
    def _():
        for which in range(2):
            near_copy(which, me).wait_recv()
            pair_copy(which).wait_send()
        swap_aux().wait()
        swap_rows().wait()

    @pl.when(sec == owner)
    def _():
        for to in range(owner):
            query_aux(to).wait_send()
            query_copy(to).wait_send()
        kept_query().wait()
        kept_query_aux().wait()

    @pl.when(sec != owner)
    def _():
        query_aux(0).wait_recv()
        query_copy(0).wait_recv()


def gather_projections(blocks, sections, shards, points, aux):
    depth, width = shards.shape[1:]
    rows = points.shape[0]
    anywhere = pl.BlockSpec(memory_space=pl.ANY)
    return pl.pallas_call(
        functools.partial(gather_kernel, blocks, sections),
        out_shape=(
            jax.ShapeDtypeStruct((2, depth * blocks, width), shards.dtype),
            jax.ShapeDtypeStruct(points.shape, points.dtype),
            jax.ShapeDtypeStruct(aux.shape, aux.dtype),
            jax.ShapeDtypeStruct((rows // 2, width), points.dtype),
            jax.ShapeDtypeStruct(aux.shape, aux.dtype),
        ),
        in_specs=[anywhere] * 3,
        out_specs=(anywhere,) * 5,
        scratch_shapes=[
            DMA((6,)),
            DMA((2, blocks)),
            DMA((2, blocks)),
            DMA((2, blocks)),
            DMA((2, blocks)),
            DMA((2, blocks)),
            DMA((2,)),
            DMA((2,)),
            DMA((2, sections)),
            DMA((2,)),
        ],
        compiler_params=pltpu.CompilerParams(
            collective_id=0, has_side_effects=True, vmem_limit_bytes=VMEM_LIMIT
        ),
    )(shards, points, aux)


def state_kernel(
    length, part_ref, out_ref, from_near, halves, landed,
    half_send, half_recv, part_send, part_recv, share_send, share_recv, across_send, across_recv,
    pair_send, pair_recv, near_send, near_recv,
):
    sec = lax.axis_index("sec")
    me = lax.axis_index("pts")
    spot, side = me // 2, lax.rem(me, 2)
    core = lax.rem(sec, 2)
    near, across = sibling_of(sec), across_of(sec)
    pair = spot * 2 + 1 - side
    mine = sec - core + side
    beyond = across_of(mine)
    beside = sibling_of(mine)
    corner = across_of(beside)
    barrier = pltpu.get_barrier_semaphore()

    def greet(**where):
        pl.semaphore_signal(barrier, inc=1, device_id=where, device_id_type=MESH)

    def after(step):
        return lax.rem(spot + step, length) * 2 + side

    greet(sec=near)
    greet(sec=across)
    greet(pts=pair)
    for step in range(1, length):
        greet(pts=after(step))
    pl.semaphore_wait(barrier, length + 2)

    half = remote(part_ref.at[1 - core], from_near, half_send, half_recv, sec=near)
    half.start()
    half.wait_recv()
    halves[...] = (part_ref[core].astype(jnp.float32) + from_near[...].astype(jnp.float32)).astype(halves.dtype)

    def part_copy(step):
        return remote(
            halves.at[lax.rem(spot + step, length)], landed.at[step], part_send.at[step], part_recv.at[step],
            pts=after(step),
        )

    def slot(section, step, parity):
        return out_ref.at[section, parity, lax.rem(spot + length - step, length)]

    def share_copy(step):
        here = slot(mine, 0, core)
        return remote(here, here, share_send.at[step], share_recv.at[step], pts=after(step))

    def arriving(step):
        here = slot(mine, step, core)
        return remote(here, here, share_send.at[step], share_recv.at[step], pts=after(step))

    def across_copy(section, step):
        here = slot(section, step, core)
        return remote(here, here, across_send.at[step], across_recv.at[step], sec=across)

    def pair_copy(kind, section, step):
        here = slot(section, step, core)
        return remote(here, here, pair_send.at[kind, step], pair_recv.at[kind, step], pts=pair)

    def near_copy(section, step, parity):
        here = slot(section, step, parity)
        return remote(here, here, near_send.at[section, step], near_recv.at[section, step], sec=near)

    for step in range(1, length):
        part_copy(step).start()
    total = halves[spot].astype(jnp.float32)
    for step in range(1, length):
        part_copy(step).wait_recv()
        total += landed[step].astype(jnp.float32)
    out_ref[mine, core, spot] = total.astype(out_ref.dtype)
    for step in range(1, length):
        share_copy(step).start()
    for step in range(length):
        if step:
            arriving(step).wait_recv()
        across_copy(mine, step).start()
        pair_copy(0, mine, step).start()
        near_copy(mine, step, core).start()
    for step in range(length):
        across_copy(beyond, step).wait_recv()
        pair_copy(1, beyond, step).start()
        near_copy(beyond, step, core).start()
        pair_copy(0, beside, step).wait_recv()
        near_copy(beside, step, core).start()
    for step in range(length):
        pair_copy(1, corner, step).wait_recv()
        near_copy(corner, step, core).start()
    for step in range(length):
        for section in (mine, beyond, beside, corner):
            near_copy(section, step, 1 - core).wait_recv()
    half.wait_send()
    for step in range(1, length):
        part_copy(step).wait_send()
        share_copy(step).wait_send()
    for step in range(length):
        across_copy(mine, step).wait_send()
        pair_copy(0, mine, step).wait_send()
        pair_copy(1, beyond, step).wait_send()
        for section in (mine, beyond, beside, corner):
            near_copy(section, step, core).wait_send()


def sum_states(blocks, sections, parts):
    length = blocks // 2
    inside = pl.BlockSpec(memory_space=pltpu.VMEM)
    slab = parts.shape[1:]
    return pl.pallas_call(
        functools.partial(state_kernel, length),
        out_shape=jax.ShapeDtypeStruct((sections,) + parts.shape, parts.dtype),
        in_specs=[inside],
        out_specs=inside,
        scratch_shapes=[
            pltpu.VMEM(slab, parts.dtype),
            pltpu.VMEM(slab, parts.dtype),
            pltpu.VMEM(slab, parts.dtype),
            DMA,
            DMA,
            DMA((length,)),
            DMA((length,)),
            DMA((length,)),
            DMA((length,)),
            DMA((length,)),
            DMA((length,)),
            DMA((2, length)),
            DMA((2, length)),
            DMA((sections, length)),
            DMA((sections, length)),
        ],
        compiler_params=pltpu.CompilerParams(
            collective_id=1, has_side_effects=True, vmem_limit_bytes=VMEM_LIMIT
        ),
    )(parts)


def feed_kernel(
    centred_ref, mixed_ref, up_ref, down_ref, out_ref,
    rows_in, sums, own, cross, to_near, from_near, to_across, from_across,
    gather_send, gather_recv, near_send, near_recv, across_send, across_recv,
):
    sec = lax.axis_index("sec")
    near, across = sibling_of(sec), across_of(sec)
    core, chip = lax.rem(sec, 2), sec // 2
    share = rows_in.shape[1]
    columns = out_ref.shape[1]
    barrier = pltpu.get_barrier_semaphore()
    for other in (near, across):
        pl.semaphore_signal(barrier, inc=1, device_id={"sec": other}, device_id_type=MESH)
    pl.semaphore_wait(barrier, 2)

    def near_rows(index):
        return remote(
            centred_ref.at[pl.ds(index * share, share)], rows_in.at[index], gather_send.at[index],
            gather_recv.at[index], sec=near,
        )

    def near_copy(block):
        return remote(to_near.at[block], from_near.at[block], near_send.at[block], near_recv.at[block], sec=near)

    def across_copy(block):
        return remote(
            to_across.at[block], from_across.at[block], across_send.at[block], across_recv.at[block], sec=across
        )

    for index in range(2):
        near_rows(index).start()
    span = 256
    steps = up_ref.shape[1] // span

    def side_of(which):
        return pl.ds(pl.multiple_of(which * 2 * columns, 2 * columns), 2 * columns)

    def run(source):
        @pl.loop(0, steps)
        def _(step):
            units = pl.ds(pl.multiple_of(step * span, span), span)
            hidden = jax.nn.gelu(
                jnp.dot(source[...], up_ref[:, units], preferred_element_type=jnp.float32), approximate=True
            ).astype(jnp.bfloat16)
            sums[...] += jnp.dot(hidden, down_ref[units, :], preferred_element_type=jnp.float32)

    def part(of):
        return sums[:, pl.ds(pl.multiple_of(of * columns, columns), columns)]

    def emit(block):
        own[block] = part(sec)
        cross[block] = part(across)
        to_near[block, 0] = part(1 - core).astype(jnp.bfloat16)
        to_near[block, 1] = part(3 - core).astype(jnp.bfloat16)
        near_copy(block).start()

    def forward(block):
        near_copy(block).wait_recv()
        to_across[block] = (cross[block] + from_near[block, 1 - chip].astype(jnp.float32)).astype(jnp.bfloat16)
        across_copy(block).start()

    order = []
    for index in range(2):
        mine, theirs = core * 2 + index, (1 - core) * 2 + index
        rows = pl.ds(index * share, share)
        sums[:, side_of(chip)] = mixed_ref[rows, side_of(chip)]
        sums[:, side_of(1 - chip)] = jnp.zeros((share, 2 * columns), jnp.float32)
        run(centred_ref.at[rows])
        emit(mine)
        near_rows(index).wait_recv()
        sums[...] = jnp.zeros_like(sums)
        run(rows_in.at[index])
        emit(theirs)
        forward(theirs)
        forward(mine)
        order += [theirs, mine]
    for block in order:
        across_copy(block).wait_recv()
        out_ref[pl.ds(pl.multiple_of(block * share, share), share), :] = (
            own[block] + from_near[block, chip].astype(jnp.float32) + from_across[block].astype(jnp.float32)
        ).astype(out_ref.dtype)
    for block in order:
        near_copy(block).wait_send()
        across_copy(block).wait_send()
    for index in range(2):
        near_rows(index).wait_send()


def feed_forward(sections, centred, mixed, up, down):
    width = centred.shape[1]
    share = centred.shape[0] // 2
    columns = width // sections
    inside = pl.BlockSpec(memory_space=pltpu.VMEM)
    half = jnp.bfloat16
    return pl.pallas_call(
        feed_kernel,
        out_shape=jax.ShapeDtypeStruct((share * 4, columns), half),
        in_specs=[inside] * 4,
        out_specs=inside,
        scratch_shapes=[
            pltpu.VMEM((2, share, width), half),
            pltpu.VMEM((share, width), jnp.float32),
            pltpu.VMEM((4, share, columns), jnp.float32),
            pltpu.VMEM((4, share, columns), jnp.float32),
            pltpu.VMEM((4, 2, share, columns), half),
            pltpu.VMEM((4, 2, share, columns), half),
            pltpu.VMEM((4, share, columns), half),
            pltpu.VMEM((4, share, columns), half),
            DMA((2,)),
            DMA((2,)),
            DMA((4,)),
            DMA((4,)),
            DMA((4,)),
            DMA((4,)),
        ],
        compiler_params=pltpu.CompilerParams(
            collective_id=2, has_side_effects=True, vmem_limit_bytes=VMEM_LIMIT
        ),
    )(centred, mixed, up, down)


def on_device(
    points,
    counts,
    input_gain,
    key_weight,
    value_weight,
    query_weight,
    output_weight,
    middle_gain,
    up_weight,
    down_weight,
):
    block = points[0]
    rows, width = block.shape
    heads = width // HEAD_DIM
    sections = lax.axis_size("sec")
    blocks = lax.axis_size("pts")
    aux = jnp.concatenate(
        [
            input_gain.reshape(heads, HEAD_DIM),
            jnp.broadcast_to(counts.astype(jnp.float32), (heads, HEAD_DIM)),
        ]
    )
    whole, taken, taken_aux, query_rows, query_aux = gather_projections(
        blocks, sections, jnp.concatenate([key_weight, value_weight]), block, aux
    )
    whole_key, whole_value = whole[0], whole[1]
    query_gain = query_aux[:heads]
    normed = layer_normalizer(
        taken.astype(jnp.float32), taken_aux[:heads].reshape(width)
    ).astype(jnp.bfloat16)
    valid = jnp.arange(rows).astype(jnp.float32) < taken_aux[heads, 0]
    key_feats = feature_map(
        jnp.dot(normed, whole_key, preferred_element_type=jnp.float32)
    ).astype(jnp.bfloat16)
    key_feats = jnp.where(valid[:, None], key_feats, jnp.zeros_like(key_feats))
    value_rows = jnp.dot(normed, whole_value, preferred_element_type=jnp.float32).astype(jnp.bfloat16)
    local_state = jnp.einsum(
        "yzl,yzn->zln",
        key_feats.reshape(rows, heads, HEAD_DIM),
        value_rows.reshape(rows, heads, HEAD_DIM),
        preferred_element_type=jnp.float32,
    ).reshape(width, HEAD_DIM)
    local_total = jnp.sum(key_feats.astype(jnp.float32), axis=0)
    slab = width // blocks
    extra = jnp.pad(local_total.reshape(blocks, 1, slab), ((0, 0), (0, EXTRA - 1), (0, HEAD_DIM - slab)))
    parts = jnp.concatenate([local_state.reshape(blocks, slab, HEAD_DIM), extra], axis=1).astype(jnp.bfloat16)
    summed = sum_states(blocks, sections, parts.reshape((2, blocks // 2) + parts.shape[1:]))
    summed = summed.reshape((sections,) + parts.shape)
    state_heads = summed[:, :, :slab].reshape(sections, heads, HEAD_DIM, HEAD_DIM)
    total_heads = summed[:, :, slab, :slab].reshape(sections, heads, HEAD_DIM)

    query_wide = query_rows.astype(jnp.float32)
    query_normed = layer_normalizer(query_wide, query_gain.reshape(width)).astype(jnp.bfloat16)
    query_feats = feature_map(
        jnp.dot(query_normed, query_weight, preferred_element_type=jnp.float32)
    ).astype(jnp.bfloat16)
    share = query_rows.shape[0]
    per_head_queries = query_feats.reshape(share, heads, HEAD_DIM)
    numerator = jnp.einsum(
        "rhk,shkv->srhv", per_head_queries, state_heads, preferred_element_type=jnp.float32
    )
    denom = jnp.einsum("rhk,shk->srh", per_head_queries, total_heads, preferred_element_type=jnp.float32)
    attended = (
        jnp.sum(numerator / denom[:, :, :, None], axis=0).reshape(share, width).astype(jnp.bfloat16)
    )
    mixed = query_wide + jnp.dot(attended, output_weight, preferred_element_type=jnp.float32)
    centred = layer_normalizer(mixed, middle_gain).astype(jnp.bfloat16)
    return feed_forward(sections, centred, mixed, up_weight, down_weight)


def solution(mesh):
    placed = (
        P("sec", "pts", None),
        P("sec", "pts"),
        P("sec", None),
        P("sec", "pts", None),
        P("sec", "pts", None),
        P(),
        P(),
        P(),
        P(None, "sec"),
        P("sec", None),
    )
    return jax.shard_map(
        on_device, mesh=mesh, in_specs=placed, out_specs=P("pts", "sec"), check_vma=False
    )
```

```python
import functools

import jax
import jax.numpy as jnp
from jax import lax
from jax.experimental import pallas as pl
from jax.experimental.pallas import tpu as pltpu
from jax.sharding import PartitionSpec as P

HEAD_DIM = 128
EXTRA = 16
MESH = pl.DeviceIdType.MESH
DMA = pltpu.SemaphoreType.DMA
VMEM_LIMIT = 48 * 1024 * 1024


def layer_normalizer(values, gain):
    mean = jnp.mean(values, axis=-1, keepdims=True)
    centred = values - mean
    spread = jnp.mean(centred * centred, axis=-1, keepdims=True)
    return centred * lax.rsqrt(spread + 1e-05) * gain


def feature_map(values):
    return jax.nn.elu(values) + 1.0


def sibling_of(sec):
    return sec + 1 - 2 * lax.rem(sec, 2)


def across_of(sec):
    return lax.rem(sec + 2, 4)


def remote(src, dst, send_sem, recv_sem, **where):
    return pltpu.make_async_remote_copy(
        src_ref=src,
        dst_ref=dst,
        send_sem=send_sem,
        recv_sem=recv_sem,
        device_id=where,
        device_id_type=MESH,
    )


def gather_kernel(
    blocks, sections, key_ref, value_ref, points_ref, aux_ref,
    whole_ref, rows_ref, rows_aux_ref, query_ref, query_aux_ref,
    local_sem, up_sem, down_sem, near_sem, pair_sem, recv_sem, swap_send, swap_recv, query_send, query_recv,
):
    length = blocks // 2
    shards = (key_ref, value_ref)
    depth = key_ref.shape[0]
    share = query_ref.shape[0]
    sec = lax.axis_index("sec")
    me = lax.axis_index("pts")
    spot, side = me // 2, lax.rem(me, 2)
    core = lax.rem(sec, 2)
    base = sec - core
    near = base + 1 - core
    pair = spot * 2 + 1 - side
    owner = sections - 1
    barrier = pltpu.get_barrier_semaphore()

    def greet(**where):
        pl.semaphore_signal(barrier, inc=1, device_id=where, device_id_type=MESH)

    for other in (near, across_of(sec), across_of(near)):
        greet(sec=other)
    for step in (1, length - 1):
        beside = lax.rem(spot + step, length) * 2 + side
        greet(pts=beside)
        greet(sec=near, pts=beside)
    greet(pts=pair)
    greet(sec=near, pts=pair)
    pl.semaphore_wait(barrier, 9)

    def place(which, index):
        return whole_ref.at[which, pl.ds(pl.multiple_of(index * depth, depth), depth)]

    def copy(which, index, sem, own, **where):
        here = place(which, index)
        return remote(
            shards[which] if own else here, here, sem.at[which, index], recv_sem.at[which, index], **where
        )

    def line_copy(which, index, step, own=False):
        where = {"sec": base + which, "pts": me + 2 * step} if own else {"pts": me + 2 * step}
        return copy(which, index, up_sem if step > 0 else down_sem, own, **where)

    def near_copy(which, index, own=False):
        return copy(which, index, near_sem, own, sec=near)

    def pair_copy(which):
        return copy(which, me, pair_sem, True, sec=base + which, pts=pair)

    def kept(which):
        return pltpu.make_async_copy(shards[which], place(which, me), local_sem.at[which])

    swap_to = {"sec": base + side, "pts": spot * 2 + core}

    def swap_rows():
        return remote(points_ref, rows_ref, swap_send.at[0], swap_recv.at[0], **swap_to)

    def swap_aux():
        return remote(aux_ref, rows_aux_ref, swap_send.at[1], swap_recv.at[1], **swap_to)

    def kept_rows():
        return pltpu.make_async_copy(points_ref, rows_ref, local_sem.at[2])

    def kept_aux():
        return pltpu.make_async_copy(aux_ref, rows_aux_ref, local_sem.at[3])

    def query_copy(to):
        return remote(
            points_ref.at[pl.ds(to % 2 * share, share)], query_ref, query_send.at[0, to], query_recv.at[0], sec=to
        )

    def query_aux(to):
        return remote(aux_ref, query_aux_ref, query_send.at[1, to], query_recv.at[1], sec=to)

    def kept_query():
        return pltpu.make_async_copy(points_ref.at[pl.ds(owner % 2 * share, share)], query_ref, local_sem.at[4])

    def kept_query_aux():
        return pltpu.make_async_copy(aux_ref, query_aux_ref, local_sem.at[5])

    @pl.when(core != side)
    def _():
        for which in range(2):
            pair_copy(which).start()

    @pl.when(core == side)
    def _():
        for which in range(2):
            @pl.when(spot < length - 1)
            def _():
                line_copy(which, me, 1, True).start()

            @pl.when(spot > 0)
            def _():
                line_copy(which, me, -1, True).start()

            near_copy(which, me, True).start()
            kept(which).start()

    @pl.when(core == side)
    def _():
        kept_aux().start()
        kept_rows().start()

    @pl.when(sec == owner)
    def _():
        for to in range(owner):
            query_aux(to).start()
            query_copy(to).start()
        kept_query().start()
        kept_query_aux().start()

    @pl.when(core != side)
    def _():
        for which in range(2):
            pair_copy(which).wait_send()
        swap_aux().start()
        swap_rows().start()

    def arrive(index, up, down):
        copy(core, index, near_sem, False, sec=near).wait_recv()
        if up:
            @pl.when(spot < length - 1)
            def _():
                line_copy(core, index, 1).start()
        if down:
            @pl.when(spot > 0)
            def _():
                line_copy(core, index, -1).start()
        near_copy(core, index).start()

    arrive(pair, True, True)
    for distance in range(1, length):
        for other in range(2):
            column = side if other == 0 else 1 - side

            @pl.when(spot - distance >= 0)
            def _():
                arrive((spot - distance) * 2 + column, True, False)

            @pl.when(spot + distance < length)
            def _():
                arrive((spot + distance) * 2 + column, False, True)

    for index in range(blocks):
        @pl.when(index != me)
        def _():
            near_copy(1 - core, index).wait_recv()
            near_copy(core, index).wait_send()

            @pl.when(jnp.logical_and(spot < length - 1, index // 2 <= spot))
            def _():
                line_copy(core, index, 1).wait_send()

            @pl.when(jnp.logical_and(spot > 0, index // 2 >= spot))
            def _():
                line_copy(core, index, -1).wait_send()

    @pl.when(core == side)
    def _():
        for which in range(2):
            @pl.when(spot < length - 1)
            def _():
                line_copy(which, me, 1, True).wait_send()

            @pl.when(spot > 0)
            def _():
                line_copy(which, me, -1, True).wait_send()

            near_copy(which, me, True).wait_send()
            kept(which).wait()
        kept_aux().wait()
        kept_rows().wait()

    @pl.when(core != side)
    def _():
        for which in range(2):
            near_copy(which, me).wait_recv()
        swap_aux().wait()
        swap_rows().wait()

    @pl.when(sec == owner)
    def _():
        for to in range(owner):
            query_aux(to).wait_send()
            query_copy(to).wait_send()
        kept_query().wait()
        kept_query_aux().wait()

    @pl.when(sec != owner)
    def _():
        query_aux(0).wait_recv()
        query_copy(0).wait_recv()


def gather_projections(blocks, sections, key, value, points, aux):
    depth, width = key.shape
    rows = points.shape[0]
    anywhere = pl.BlockSpec(memory_space=pl.ANY)
    return pl.pallas_call(
        functools.partial(gather_kernel, blocks, sections),
        out_shape=(
            jax.ShapeDtypeStruct((2, depth * blocks, width), key.dtype),
            jax.ShapeDtypeStruct(points.shape, points.dtype),
            jax.ShapeDtypeStruct(aux.shape, aux.dtype),
            jax.ShapeDtypeStruct((rows // 2, width), points.dtype),
            jax.ShapeDtypeStruct(aux.shape, aux.dtype),
        ),
        in_specs=[anywhere] * 4,
        out_specs=(anywhere,) * 5,
        scratch_shapes=[
            DMA((6,)),
            DMA((2, blocks)),
            DMA((2, blocks)),
            DMA((2, blocks)),
            DMA((2, blocks)),
            DMA((2, blocks)),
            DMA((2,)),
            DMA((2,)),
            DMA((2, sections)),
            DMA((2,)),
        ],
        compiler_params=pltpu.CompilerParams(collective_id=0, has_side_effects=True),
    )(key, value, points, aux)


def state_kernel(
    length, part_ref, out_ref, from_near, halves, landed,
    half_send, half_recv, part_send, part_recv, share_send, share_recv, across_send, across_recv,
    pair_send, pair_recv, near_send, near_recv,
):
    sec = lax.axis_index("sec")
    me = lax.axis_index("pts")
    spot, side = me // 2, lax.rem(me, 2)
    core = lax.rem(sec, 2)
    near, across = sibling_of(sec), across_of(sec)
    pair = spot * 2 + 1 - side
    mine = sec - core + side
    beyond = across_of(mine)
    beside = sibling_of(mine)
    corner = across_of(beside)
    barrier = pltpu.get_barrier_semaphore()

    def greet(**where):
        pl.semaphore_signal(barrier, inc=1, device_id=where, device_id_type=MESH)

    def after(step):
        return lax.rem(spot + step, length) * 2 + side

    greet(sec=near)
    greet(sec=across)
    greet(pts=pair)
    for step in range(1, length):
        greet(pts=after(step))
    pl.semaphore_wait(barrier, length + 2)

    half = remote(part_ref.at[1 - core], from_near, half_send, half_recv, sec=near)
    half.start()
    half.wait_recv()
    halves[...] = (part_ref[core].astype(jnp.float32) + from_near[...].astype(jnp.float32)).astype(halves.dtype)

    def part_copy(step):
        return remote(
            halves.at[lax.rem(spot + step, length)], landed.at[step], part_send.at[step], part_recv.at[step],
            pts=after(step),
        )

    def slot(section, step, parity):
        return out_ref.at[section, parity, lax.rem(spot + length - step, length)]

    def share_copy(step):
        here = slot(mine, 0, core)
        return remote(here, here, share_send.at[step], share_recv.at[step], pts=after(step))

    def arriving(step):
        here = slot(mine, step, core)
        return remote(here, here, share_send.at[step], share_recv.at[step], pts=after(step))

    def across_copy(section, step):
        here = slot(section, step, core)
        return remote(here, here, across_send.at[step], across_recv.at[step], sec=across)

    def pair_copy(kind, section, step):
        here = slot(section, step, core)
        return remote(here, here, pair_send.at[kind, step], pair_recv.at[kind, step], pts=pair)

    def near_copy(section, step, parity):
        here = slot(section, step, parity)
        return remote(here, here, near_send.at[section, step], near_recv.at[section, step], sec=near)

    for step in range(1, length):
        part_copy(step).start()
    total = halves[spot].astype(jnp.float32)
    for step in range(1, length):
        part_copy(step).wait_recv()
        total += landed[step].astype(jnp.float32)
    out_ref[mine, core, spot] = total.astype(out_ref.dtype)
    for step in range(1, length):
        share_copy(step).start()
    for step in range(length):
        if step:
            arriving(step).wait_recv()
        across_copy(mine, step).start()
        pair_copy(0, mine, step).start()
        near_copy(mine, step, core).start()
    for step in range(length):
        across_copy(beyond, step).wait_recv()
        pair_copy(1, beyond, step).start()
        near_copy(beyond, step, core).start()
        pair_copy(0, beside, step).wait_recv()
        near_copy(beside, step, core).start()
    for step in range(length):
        pair_copy(1, corner, step).wait_recv()
        near_copy(corner, step, core).start()
    for step in range(length):
        for section in (mine, beyond, beside, corner):
            near_copy(section, step, 1 - core).wait_recv()
    half.wait_send()
    for step in range(1, length):
        part_copy(step).wait_send()
        share_copy(step).wait_send()
    for step in range(length):
        across_copy(mine, step).wait_send()
        pair_copy(0, mine, step).wait_send()
        pair_copy(1, beyond, step).wait_send()
        for section in (mine, beyond, beside, corner):
            near_copy(section, step, core).wait_send()


def sum_states(blocks, sections, parts):
    length = blocks // 2
    inside = pl.BlockSpec(memory_space=pltpu.VMEM)
    slab = parts.shape[1:]
    return pl.pallas_call(
        functools.partial(state_kernel, length),
        out_shape=jax.ShapeDtypeStruct((sections,) + parts.shape, parts.dtype),
        in_specs=[inside],
        out_specs=inside,
        scratch_shapes=[
            pltpu.VMEM(slab, parts.dtype),
            pltpu.VMEM(slab, parts.dtype),
            pltpu.VMEM(slab, parts.dtype),
            DMA,
            DMA,
            DMA((length,)),
            DMA((length,)),
            DMA((length,)),
            DMA((length,)),
            DMA((length,)),
            DMA((length,)),
            DMA((2, length)),
            DMA((2, length)),
            DMA((sections, length)),
            DMA((sections, length)),
        ],
        compiler_params=pltpu.CompilerParams(
            collective_id=1, has_side_effects=True, vmem_limit_bytes=VMEM_LIMIT
        ),
    )(parts)


def feed_kernel(
    centred_ref, mixed_ref, up_ref, down_ref, out_ref,
    rows_in, hidden, sums, own, cross, to_near, from_near, to_across, from_across,
    gather_send, gather_recv, near_send, near_recv, across_send, across_recv,
):
    sec = lax.axis_index("sec")
    near, across = sibling_of(sec), across_of(sec)
    core, chip = lax.rem(sec, 2), sec // 2
    share = rows_in.shape[1]
    columns = out_ref.shape[1]
    barrier = pltpu.get_barrier_semaphore()
    for other in (near, across):
        pl.semaphore_signal(barrier, inc=1, device_id={"sec": other}, device_id_type=MESH)
    pl.semaphore_wait(barrier, 2)

    def near_rows(index):
        return remote(
            centred_ref.at[pl.ds(index * share, share)], rows_in.at[index], gather_send.at[index],
            gather_recv.at[index], sec=near,
        )

    def near_copy(block):
        return remote(to_near.at[block], from_near.at[block], near_send.at[block], near_recv.at[block], sec=near)

    def across_copy(block):
        return remote(
            to_across.at[block], from_across.at[block], across_send.at[block], across_recv.at[block], sec=across
        )

    for index in range(2):
        near_rows(index).start()
    span = 512
    spans = [pl.ds(start, span) for start in range(0, up_ref.shape[1], span)]

    def side_of(which):
        return pl.ds(pl.multiple_of(which * 2 * columns, 2 * columns), 2 * columns)

    def run(source):
        for units in spans:
            hidden[:, units] = jax.nn.gelu(
                jnp.dot(source[...], up_ref[:, units], preferred_element_type=jnp.float32), approximate=True
            ).astype(hidden.dtype)
        for outs in spans:
            sums[:, outs] = jnp.dot(hidden[...], down_ref[:, outs], preferred_element_type=jnp.float32)

    def part(of):
        return sums[:, pl.ds(pl.multiple_of(of * columns, columns), columns)]

    def emit(block):
        own[block] = part(sec)
        cross[block] = part(across)
        to_near[block, 0] = part(1 - core).astype(jnp.bfloat16)
        to_near[block, 1] = part(3 - core).astype(jnp.bfloat16)
        near_copy(block).start()

    def forward(block):
        near_copy(block).wait_recv()
        to_across[block] = (cross[block] + from_near[block, 1 - chip].astype(jnp.float32)).astype(jnp.bfloat16)
        across_copy(block).start()

    order = []
    for index in range(2):
        mine, theirs = core * 2 + index, (1 - core) * 2 + index
        rows = pl.ds(index * share, share)
        run(centred_ref.at[rows])
        sums[:, side_of(chip)] += mixed_ref[rows, side_of(chip)]
        emit(mine)
        near_rows(index).wait_recv()
        run(rows_in.at[index])
        emit(theirs)
        forward(theirs)
        forward(mine)
        order += [theirs, mine]
    for block in order:
        across_copy(block).wait_recv()
        out_ref[pl.ds(pl.multiple_of(block * share, share), share), :] = (
            own[block] + from_near[block, chip].astype(jnp.float32) + from_across[block].astype(jnp.float32)
        ).astype(out_ref.dtype)
    for block in order:
        near_copy(block).wait_send()
        across_copy(block).wait_send()
    for index in range(2):
        near_rows(index).wait_send()


def feed_forward(sections, centred, mixed, up, down):
    width = centred.shape[1]
    share = centred.shape[0] // 2
    columns = width // sections
    inside = pl.BlockSpec(memory_space=pltpu.VMEM)
    half = jnp.bfloat16
    return pl.pallas_call(
        feed_kernel,
        out_shape=jax.ShapeDtypeStruct((share * 4, columns), half),
        in_specs=[inside] * 4,
        out_specs=inside,
        scratch_shapes=[
            pltpu.VMEM((2, share, width), half),
            pltpu.VMEM((share, up.shape[1]), half),
            pltpu.VMEM((share, width), jnp.float32),
            pltpu.VMEM((4, share, columns), jnp.float32),
            pltpu.VMEM((4, share, columns), jnp.float32),
            pltpu.VMEM((4, 2, share, columns), half),
            pltpu.VMEM((4, 2, share, columns), half),
            pltpu.VMEM((4, share, columns), half),
            pltpu.VMEM((4, share, columns), half),
            DMA((2,)),
            DMA((2,)),
            DMA((4,)),
            DMA((4,)),
            DMA((4,)),
            DMA((4,)),
        ],
        compiler_params=pltpu.CompilerParams(
            collective_id=2, has_side_effects=True, vmem_limit_bytes=VMEM_LIMIT
        ),
    )(centred, mixed, up, down)


def on_device(
    points,
    counts,
    input_gain,
    key_weight,
    value_weight,
    query_weight,
    output_weight,
    middle_gain,
    up_weight,
    down_weight,
):
    block = points[0]
    rows, width = block.shape
    heads = width // HEAD_DIM
    sections = lax.axis_size("sec")
    blocks = lax.axis_size("pts")
    aux = jnp.concatenate(
        [
            input_gain.reshape(heads, HEAD_DIM),
            jnp.broadcast_to(counts.astype(jnp.float32), (heads, HEAD_DIM)),
        ]
    )
    whole, taken, taken_aux, query_rows, query_aux = gather_projections(
        blocks, sections, key_weight[0], value_weight[0], block, aux
    )
    whole_key, whole_value = whole[0], whole[1]
    query_gain = query_aux[:heads]
    normed = layer_normalizer(
        taken.astype(jnp.float32), taken_aux[:heads].reshape(width)
    ).astype(jnp.bfloat16)
    valid = jnp.arange(rows).astype(jnp.float32) < taken_aux[heads, 0]
    key_feats = feature_map(
        jnp.dot(normed, whole_key, preferred_element_type=jnp.float32)
    ).astype(jnp.bfloat16)
    key_feats = jnp.where(valid[:, None], key_feats, jnp.zeros_like(key_feats))
    value_rows = jnp.dot(normed, whole_value, preferred_element_type=jnp.float32).astype(jnp.bfloat16)
    local_state = jnp.einsum(
        "yzl,yzn->zln",
        key_feats.reshape(rows, heads, HEAD_DIM),
        value_rows.reshape(rows, heads, HEAD_DIM),
        preferred_element_type=jnp.float32,
    ).reshape(width, HEAD_DIM)
    local_total = jnp.sum(key_feats.astype(jnp.float32), axis=0)
    slab = width // blocks
    extra = jnp.pad(local_total.reshape(blocks, 1, slab), ((0, 0), (0, EXTRA - 1), (0, HEAD_DIM - slab)))
    parts = jnp.concatenate([local_state.reshape(blocks, slab, HEAD_DIM), extra], axis=1).astype(jnp.bfloat16)
    summed = sum_states(blocks, sections, parts.reshape((2, blocks // 2) + parts.shape[1:]))
    summed = summed.reshape((sections,) + parts.shape)
    state_heads = summed[:, :, :slab].reshape(sections, heads, HEAD_DIM, HEAD_DIM)
    total_heads = summed[:, :, slab, :slab].reshape(sections, heads, HEAD_DIM)

    query_wide = query_rows.astype(jnp.float32)
    query_normed = layer_normalizer(query_wide, query_gain.reshape(width)).astype(jnp.bfloat16)
    query_feats = feature_map(
        jnp.dot(query_normed, query_weight, preferred_element_type=jnp.float32)
    ).astype(jnp.bfloat16)
    share = query_rows.shape[0]
    per_head_queries = query_feats.reshape(share, heads, HEAD_DIM)
    numerator = jnp.einsum(
        "rhk,shkv->srhv", per_head_queries, state_heads, preferred_element_type=jnp.float32
    )
    denom = jnp.einsum("rhk,shk->srh", per_head_queries, total_heads, preferred_element_type=jnp.float32)
    attended = (
        jnp.sum(numerator / denom[:, :, :, None], axis=0).reshape(share, width).astype(jnp.bfloat16)
    )
    mixed = query_wide + jnp.dot(attended, output_weight, preferred_element_type=jnp.float32)
    centred = layer_normalizer(mixed, middle_gain).astype(jnp.bfloat16)
    return feed_forward(sections, centred, mixed, up_weight, down_weight)


def solution(mesh):
    placed = (
        P("sec", "pts", None),
        P("sec", "pts"),
        P("sec", None),
        P("sec", "pts", None),
        P("sec", "pts", None),
        P(),
        P(),
        P(),
        P(None, "sec"),
        P("sec", None),
    )
    return jax.shard_map(
        on_device, mesh=mesh, in_specs=placed, out_specs=P("pts", "sec"), check_vma=False
    )
```

```python
import functools

import jax
import jax.numpy as jnp
from jax import lax
from jax.experimental import pallas as pl
from jax.experimental.pallas import tpu as pltpu
from jax.sharding import PartitionSpec as P

HEAD_DIM = 128
EXTRA = 16
MESH = pl.DeviceIdType.MESH
DMA = pltpu.SemaphoreType.DMA
VMEM_LIMIT = 48 * 1024 * 1024


def layer_normalizer(values, gain):
    mean = jnp.mean(values, axis=-1, keepdims=True)
    centred = values - mean
    spread = jnp.mean(centred * centred, axis=-1, keepdims=True)
    return centred * lax.rsqrt(spread + 1e-05) * gain


def feature_map(values):
    return jax.nn.elu(values) + 1.0


def sibling_of(sec):
    return sec + 1 - 2 * lax.rem(sec, 2)


def across_of(sec):
    return lax.rem(sec + 2, 4)


def remote(src, dst, send_sem, recv_sem, **where):
    return pltpu.make_async_remote_copy(
        src_ref=src,
        dst_ref=dst,
        send_sem=send_sem,
        recv_sem=recv_sem,
        device_id=where,
        device_id_type=MESH,
    )


def gather_kernel(
    blocks, sections, key_ref, value_ref, points_ref, aux_ref,
    whole_ref, rows_ref, rows_aux_ref, query_ref, query_aux_ref,
    local_sem, up_sem, down_sem, near_sem, pair_sem, recv_sem, swap_send, swap_recv, query_send, query_recv,
):
    length = blocks // 2
    shards = (key_ref, value_ref)
    depth = key_ref.shape[0]
    share = query_ref.shape[0]
    sec = lax.axis_index("sec")
    me = lax.axis_index("pts")
    spot, side = me // 2, lax.rem(me, 2)
    core = lax.rem(sec, 2)
    base = sec - core
    near = base + 1 - core
    pair = spot * 2 + 1 - side
    owner = sections - 1
    barrier = pltpu.get_barrier_semaphore()

    def greet(**where):
        pl.semaphore_signal(barrier, inc=1, device_id=where, device_id_type=MESH)

    for other in (near, across_of(sec), across_of(near)):
        greet(sec=other)
    for step in (1, length - 1):
        beside = lax.rem(spot + step, length) * 2 + side
        greet(pts=beside)
        greet(sec=near, pts=beside)
    greet(pts=pair)
    greet(sec=near, pts=pair)
    pl.semaphore_wait(barrier, 9)

    def place(which, index):
        return whole_ref.at[which, pl.ds(pl.multiple_of(index * depth, depth), depth)]

    def copy(which, index, sem, own, **where):
        here = place(which, index)
        return remote(
            shards[which] if own else here, here, sem.at[which, index], recv_sem.at[which, index], **where
        )

    def line_copy(which, index, step, own=False):
        where = {"sec": base + which, "pts": me + 2 * step} if own else {"pts": me + 2 * step}
        return copy(which, index, up_sem if step > 0 else down_sem, own, **where)

    def near_copy(which, index, own=False):
        return copy(which, index, near_sem, own, sec=near)

    def pair_copy(which):
        return copy(which, me, pair_sem, True, sec=base + which, pts=pair)

    def kept(which):
        return pltpu.make_async_copy(shards[which], place(which, me), local_sem.at[which])

    swap_to = {"sec": base + side, "pts": spot * 2 + core}

    def swap_rows():
        return remote(points_ref, rows_ref, swap_send.at[0], swap_recv.at[0], **swap_to)

    def swap_aux():
        return remote(aux_ref, rows_aux_ref, swap_send.at[1], swap_recv.at[1], **swap_to)

    def kept_rows():
        return pltpu.make_async_copy(points_ref, rows_ref, local_sem.at[2])

    def kept_aux():
        return pltpu.make_async_copy(aux_ref, rows_aux_ref, local_sem.at[3])

    def query_copy(to):
        return remote(
            points_ref.at[pl.ds(to % 2 * share, share)], query_ref, query_send.at[0, to], query_recv.at[0], sec=to
        )

    def query_aux(to):
        return remote(aux_ref, query_aux_ref, query_send.at[1, to], query_recv.at[1], sec=to)

    def kept_query():
        return pltpu.make_async_copy(points_ref.at[pl.ds(owner % 2 * share, share)], query_ref, local_sem.at[4])

    def kept_query_aux():
        return pltpu.make_async_copy(aux_ref, query_aux_ref, local_sem.at[5])

    @pl.when(core != side)
    def _():
        for which in range(2):
            pair_copy(which).start()

    @pl.when(core == side)
    def _():
        for which in range(2):
            @pl.when(spot < length - 1)
            def _():
                line_copy(which, me, 1, True).start()

            @pl.when(spot > 0)
            def _():
                line_copy(which, me, -1, True).start()

            near_copy(which, me, True).start()
            kept(which).start()

    @pl.when(core == side)
    def _():
        kept_aux().start()
        kept_rows().start()

    @pl.when(sec == owner)
    def _():
        for to in range(owner):
            query_aux(to).start()
            query_copy(to).start()
        kept_query().start()
        kept_query_aux().start()

    @pl.when(core != side)
    def _():
        for which in range(2):
            pair_copy(which).wait_send()
        swap_aux().start()
        swap_rows().start()

    def arrive(index, up, down):
        copy(core, index, near_sem, False, sec=near).wait_recv()
        if up:
            @pl.when(spot < length - 1)
            def _():
                line_copy(core, index, 1).start()
        if down:
            @pl.when(spot > 0)
            def _():
                line_copy(core, index, -1).start()
        near_copy(core, index).start()

    arrive(pair, True, True)
    for distance in range(1, length):
        for other in range(2):
            column = side if other == 0 else 1 - side

            @pl.when(spot - distance >= 0)
            def _():
                arrive((spot - distance) * 2 + column, True, False)

            @pl.when(spot + distance < length)
            def _():
                arrive((spot + distance) * 2 + column, False, True)

    for index in range(blocks):
        @pl.when(index != me)
        def _():
            near_copy(1 - core, index).wait_recv()
            near_copy(core, index).wait_send()

            @pl.when(jnp.logical_and(spot < length - 1, index // 2 <= spot))
            def _():
                line_copy(core, index, 1).wait_send()

            @pl.when(jnp.logical_and(spot > 0, index // 2 >= spot))
            def _():
                line_copy(core, index, -1).wait_send()

    @pl.when(core == side)
    def _():
        for which in range(2):
            @pl.when(spot < length - 1)
            def _():
                line_copy(which, me, 1, True).wait_send()

            @pl.when(spot > 0)
            def _():
                line_copy(which, me, -1, True).wait_send()

            near_copy(which, me, True).wait_send()
            kept(which).wait()
        kept_aux().wait()
        kept_rows().wait()

    @pl.when(core != side)
    def _():
        for which in range(2):
            near_copy(which, me).wait_recv()
        swap_aux().wait()
        swap_rows().wait()

    @pl.when(sec == owner)
    def _():
        for to in range(owner):
            query_aux(to).wait_send()
            query_copy(to).wait_send()
        kept_query().wait()
        kept_query_aux().wait()

    @pl.when(sec != owner)
    def _():
        query_aux(0).wait_recv()
        query_copy(0).wait_recv()


def gather_projections(blocks, sections, key, value, points, aux):
    depth, width = key.shape
    rows = points.shape[0]
    anywhere = pl.BlockSpec(memory_space=pl.ANY)
    return pl.pallas_call(
        functools.partial(gather_kernel, blocks, sections),
        out_shape=(
            jax.ShapeDtypeStruct((2, depth * blocks, width), key.dtype),
            jax.ShapeDtypeStruct(points.shape, points.dtype),
            jax.ShapeDtypeStruct(aux.shape, aux.dtype),
            jax.ShapeDtypeStruct((rows // 2, width), points.dtype),
            jax.ShapeDtypeStruct(aux.shape, aux.dtype),
        ),
        in_specs=[anywhere] * 4,
        out_specs=(anywhere,) * 5,
        scratch_shapes=[
            DMA((6,)),
            DMA((2, blocks)),
            DMA((2, blocks)),
            DMA((2, blocks)),
            DMA((2, blocks)),
            DMA((2, blocks)),
            DMA((2,)),
            DMA((2,)),
            DMA((2, sections)),
            DMA((2,)),
        ],
        compiler_params=pltpu.CompilerParams(
            collective_id=0, has_side_effects=True, vmem_limit_bytes=VMEM_LIMIT
        ),
    )(key, value, points, aux)


def state_kernel(
    length, part_ref, out_ref, from_near, halves, landed,
    half_send, half_recv, part_send, part_recv, share_send, share_recv, across_send, across_recv,
    pair_send, pair_recv, near_send, near_recv,
):
    sec = lax.axis_index("sec")
    me = lax.axis_index("pts")
    spot, side = me // 2, lax.rem(me, 2)
    core = lax.rem(sec, 2)
    near, across = sibling_of(sec), across_of(sec)
    pair = spot * 2 + 1 - side
    mine = sec - core + side
    beyond = across_of(mine)
    beside = sibling_of(mine)
    corner = across_of(beside)
    barrier = pltpu.get_barrier_semaphore()

    def greet(**where):
        pl.semaphore_signal(barrier, inc=1, device_id=where, device_id_type=MESH)

    def after(step):
        return lax.rem(spot + step, length) * 2 + side

    greet(sec=near)
    greet(sec=across)
    greet(pts=pair)
    for step in range(1, length):
        greet(pts=after(step))
    pl.semaphore_wait(barrier, length + 2)

    half = remote(part_ref.at[1 - core], from_near, half_send, half_recv, sec=near)
    half.start()
    half.wait_recv()
    halves[...] = (part_ref[core].astype(jnp.float32) + from_near[...].astype(jnp.float32)).astype(halves.dtype)

    def part_copy(step):
        return remote(
            halves.at[lax.rem(spot + step, length)], landed.at[step], part_send.at[step], part_recv.at[step],
            pts=after(step),
        )

    def slot(section, step, parity):
        return out_ref.at[section, parity, lax.rem(spot + length - step, length)]

    def share_copy(step):
        here = slot(mine, 0, core)
        return remote(here, here, share_send.at[step], share_recv.at[step], pts=after(step))

    def arriving(step):
        here = slot(mine, step, core)
        return remote(here, here, share_send.at[step], share_recv.at[step], pts=after(step))

    def across_copy(section, step):
        here = slot(section, step, core)
        return remote(here, here, across_send.at[step], across_recv.at[step], sec=across)

    def pair_copy(kind, section, step):
        here = slot(section, step, core)
        return remote(here, here, pair_send.at[kind, step], pair_recv.at[kind, step], pts=pair)

    def near_copy(section, step, parity):
        here = slot(section, step, parity)
        return remote(here, here, near_send.at[section, step], near_recv.at[section, step], sec=near)

    for step in range(1, length):
        part_copy(step).start()
    total = halves[spot].astype(jnp.float32)
    for step in range(1, length):
        part_copy(step).wait_recv()
        total += landed[step].astype(jnp.float32)
    out_ref[mine, core, spot] = total.astype(out_ref.dtype)
    for step in range(1, length):
        share_copy(step).start()
    for step in range(length):
        if step:
            arriving(step).wait_recv()
        across_copy(mine, step).start()
        pair_copy(0, mine, step).start()
        near_copy(mine, step, core).start()
    for step in range(length):
        across_copy(beyond, step).wait_recv()
        pair_copy(1, beyond, step).start()
        near_copy(beyond, step, core).start()
        pair_copy(0, beside, step).wait_recv()
        near_copy(beside, step, core).start()
    for step in range(length):
        pair_copy(1, corner, step).wait_recv()
        near_copy(corner, step, core).start()
    for step in range(length):
        for section in (mine, beyond, beside, corner):
            near_copy(section, step, 1 - core).wait_recv()
    half.wait_send()
    for step in range(1, length):
        part_copy(step).wait_send()
        share_copy(step).wait_send()
    for step in range(length):
        across_copy(mine, step).wait_send()
        pair_copy(0, mine, step).wait_send()
        pair_copy(1, beyond, step).wait_send()
        for section in (mine, beyond, beside, corner):
            near_copy(section, step, core).wait_send()


def sum_states(blocks, sections, parts):
    length = blocks // 2
    inside = pl.BlockSpec(memory_space=pltpu.VMEM)
    slab = parts.shape[1:]
    return pl.pallas_call(
        functools.partial(state_kernel, length),
        out_shape=jax.ShapeDtypeStruct((sections,) + parts.shape, parts.dtype),
        in_specs=[inside],
        out_specs=inside,
        scratch_shapes=[
            pltpu.VMEM(slab, parts.dtype),
            pltpu.VMEM(slab, parts.dtype),
            pltpu.VMEM(slab, parts.dtype),
            DMA,
            DMA,
            DMA((length,)),
            DMA((length,)),
            DMA((length,)),
            DMA((length,)),
            DMA((length,)),
            DMA((length,)),
            DMA((2, length)),
            DMA((2, length)),
            DMA((sections, length)),
            DMA((sections, length)),
        ],
        compiler_params=pltpu.CompilerParams(
            collective_id=1, has_side_effects=True, vmem_limit_bytes=VMEM_LIMIT
        ),
    )(parts)


def feed_kernel(
    centred_ref, mixed_ref, up_ref, down_ref, out_ref,
    rows_in, hidden, sums, own, cross, to_near, from_near, to_across, from_across,
    gather_send, gather_recv, near_send, near_recv, across_send, across_recv,
):
    sec = lax.axis_index("sec")
    near, across = sibling_of(sec), across_of(sec)
    core, chip = lax.rem(sec, 2), sec // 2
    share = rows_in.shape[1]
    columns = out_ref.shape[1]
    barrier = pltpu.get_barrier_semaphore()
    for other in (near, across):
        pl.semaphore_signal(barrier, inc=1, device_id={"sec": other}, device_id_type=MESH)
    pl.semaphore_wait(barrier, 2)

    def near_rows(index):
        return remote(
            centred_ref.at[pl.ds(index * share, share)], rows_in.at[index], gather_send.at[index],
            gather_recv.at[index], sec=near,
        )

    def near_copy(block):
        return remote(to_near.at[block], from_near.at[block], near_send.at[block], near_recv.at[block], sec=near)

    def across_copy(block):
        return remote(
            to_across.at[block], from_across.at[block], across_send.at[block], across_recv.at[block], sec=across
        )

    for index in range(2):
        near_rows(index).start()
    span = 512
    spans = [pl.ds(start, span) for start in range(0, up_ref.shape[1], span)]

    def side_of(which):
        return pl.ds(pl.multiple_of(which * 2 * columns, 2 * columns), 2 * columns)

    def run(source):
        for units in spans:
            hidden[:, units] = jax.nn.gelu(
                jnp.dot(source[...], up_ref[:, units], preferred_element_type=jnp.float32), approximate=True
            ).astype(hidden.dtype)
        for outs in spans:
            sums[:, outs] = jnp.dot(hidden[...], down_ref[:, outs], preferred_element_type=jnp.float32)

    def part(of):
        return sums[:, pl.ds(pl.multiple_of(of * columns, columns), columns)]

    def emit(block):
        own[block] = part(sec)
        cross[block] = part(across)
        to_near[block, 0] = part(1 - core).astype(jnp.bfloat16)
        to_near[block, 1] = part(3 - core).astype(jnp.bfloat16)
        near_copy(block).start()

    def forward(block):
        near_copy(block).wait_recv()
        to_across[block] = (cross[block] + from_near[block, 1 - chip].astype(jnp.float32)).astype(jnp.bfloat16)
        across_copy(block).start()

    order = []
    for index in range(2):
        mine, theirs = core * 2 + index, (1 - core) * 2 + index
        rows = pl.ds(index * share, share)
        run(centred_ref.at[rows])
        sums[:, side_of(chip)] += mixed_ref[rows, side_of(chip)]
        emit(mine)
        near_rows(index).wait_recv()
        run(rows_in.at[index])
        emit(theirs)
        forward(theirs)
        forward(mine)
        order += [theirs, mine]
    for block in order:
        across_copy(block).wait_recv()
        out_ref[pl.ds(pl.multiple_of(block * share, share), share), :] = (
            own[block] + from_near[block, chip].astype(jnp.float32) + from_across[block].astype(jnp.float32)
        ).astype(out_ref.dtype)
    for block in order:
        near_copy(block).wait_send()
        across_copy(block).wait_send()
    for index in range(2):
        near_rows(index).wait_send()


def feed_forward(sections, centred, mixed, up, down):
    width = centred.shape[1]
    share = centred.shape[0] // 2
    columns = width // sections
    inside = pl.BlockSpec(memory_space=pltpu.VMEM)
    half = jnp.bfloat16
    return pl.pallas_call(
        feed_kernel,
        out_shape=jax.ShapeDtypeStruct((share * 4, columns), half),
        in_specs=[inside] * 4,
        out_specs=inside,
        scratch_shapes=[
            pltpu.VMEM((2, share, width), half),
            pltpu.VMEM((share, up.shape[1]), half),
            pltpu.VMEM((share, width), jnp.float32),
            pltpu.VMEM((4, share, columns), jnp.float32),
            pltpu.VMEM((4, share, columns), jnp.float32),
            pltpu.VMEM((4, 2, share, columns), half),
            pltpu.VMEM((4, 2, share, columns), half),
            pltpu.VMEM((4, share, columns), half),
            pltpu.VMEM((4, share, columns), half),
            DMA((2,)),
            DMA((2,)),
            DMA((4,)),
            DMA((4,)),
            DMA((4,)),
            DMA((4,)),
        ],
        compiler_params=pltpu.CompilerParams(
            collective_id=2, has_side_effects=True, vmem_limit_bytes=VMEM_LIMIT
        ),
    )(centred, mixed, up, down)


def on_device(
    points,
    counts,
    input_gain,
    key_weight,
    value_weight,
    query_weight,
    output_weight,
    middle_gain,
    up_weight,
    down_weight,
):
    block = points[0]
    rows, width = block.shape
    heads = width // HEAD_DIM
    sections = lax.axis_size("sec")
    blocks = lax.axis_size("pts")
    aux = jnp.concatenate(
        [
            input_gain.reshape(heads, HEAD_DIM),
            jnp.broadcast_to(counts.astype(jnp.float32), (heads, HEAD_DIM)),
        ]
    )
    whole, taken, taken_aux, query_rows, query_aux = gather_projections(
        blocks, sections, key_weight[0], value_weight[0], block, aux
    )
    whole_key, whole_value = whole[0], whole[1]
    query_gain = query_aux[:heads]
    normed = layer_normalizer(
        taken.astype(jnp.float32), taken_aux[:heads].reshape(width)
    ).astype(jnp.bfloat16)
    valid = jnp.arange(rows).astype(jnp.float32) < taken_aux[heads, 0]
    key_feats = feature_map(
        jnp.dot(normed, whole_key, preferred_element_type=jnp.float32)
    ).astype(jnp.bfloat16)
    key_feats = jnp.where(valid[:, None], key_feats, jnp.zeros_like(key_feats))
    value_rows = jnp.dot(normed, whole_value, preferred_element_type=jnp.float32).astype(jnp.bfloat16)
    local_state = jnp.einsum(
        "yzl,yzn->zln",
        key_feats.reshape(rows, heads, HEAD_DIM),
        value_rows.reshape(rows, heads, HEAD_DIM),
        preferred_element_type=jnp.float32,
    ).reshape(width, HEAD_DIM)
    local_total = jnp.sum(key_feats.astype(jnp.float32), axis=0)
    slab = width // blocks
    extra = jnp.pad(local_total.reshape(blocks, 1, slab), ((0, 0), (0, EXTRA - 1), (0, HEAD_DIM - slab)))
    parts = jnp.concatenate([local_state.reshape(blocks, slab, HEAD_DIM), extra], axis=1).astype(jnp.bfloat16)
    summed = sum_states(blocks, sections, parts.reshape((2, blocks // 2) + parts.shape[1:]))
    summed = summed.reshape((sections,) + parts.shape)
    state_heads = summed[:, :, :slab].reshape(sections, heads, HEAD_DIM, HEAD_DIM)
    total_heads = summed[:, :, slab, :slab].reshape(sections, heads, HEAD_DIM)

    query_wide = query_rows.astype(jnp.float32)
    query_normed = layer_normalizer(query_wide, query_gain.reshape(width)).astype(jnp.bfloat16)
    query_feats = feature_map(
        jnp.dot(query_normed, query_weight, preferred_element_type=jnp.float32)
    ).astype(jnp.bfloat16)
    share = query_rows.shape[0]
    per_head_queries = query_feats.reshape(share, heads, HEAD_DIM)
    numerator = jnp.einsum(
        "rhk,shkv->srhv", per_head_queries, state_heads, preferred_element_type=jnp.float32
    )
    denom = jnp.einsum("rhk,shk->srh", per_head_queries, total_heads, preferred_element_type=jnp.float32)
    attended = (
        jnp.sum(numerator / denom[:, :, :, None], axis=0).reshape(share, width).astype(jnp.bfloat16)
    )
    mixed = query_wide + jnp.dot(attended, output_weight, preferred_element_type=jnp.float32)
    centred = layer_normalizer(mixed, middle_gain).astype(jnp.bfloat16)
    return feed_forward(sections, centred, mixed, up_weight, down_weight)


def solution(mesh):
    placed = (
        P("sec", "pts", None),
        P("sec", "pts"),
        P("sec", None),
        P("sec", "pts", None),
        P("sec", "pts", None),
        P(),
        P(),
        P(),
        P(None, "sec"),
        P("sec", None),
    )
    return jax.shard_map(
        on_device, mesh=mesh, in_specs=placed, out_specs=P("pts", "sec"), check_vma=False
    )
```
